256 devices in a mesh: dp: 16 (over y_hi, x, core), mp: 16 (over y_lo, z).
Axes of the slice: x: 4, y: 4 (y_hi: 2, y_lo: 2; y = y_hi * 2 + y_lo), z: 8, core: 2. Of those that a mesh axis runs over, the one named last changes fastest.
Arguments:
- activations: bfloat16 [4096, 4096], P('dp', 'mp'), may hold values from -6 to 6
- output_grads: bfloat16 [4096, 32768], P('dp', 'mp'), may hold values from -0.09375 to 0.09375
- owners: int32 [16, 16], replicated, may hold values from 0 to 15, as said below
- statistics: float32 [16, 16, 1024, 1024], P('mp', 'dp'), may hold values from -3 to 8
- inv_roots: bfloat16 [16, 16, 1024, 1024], P('mp', 'dp'), may hold values from -3 to 6
Outputs:
- new_statistics: float32 [16, 16, 1024, 1024], P('mp', 'dp')
- preconditioned: bfloat16 [4096, 32768], P('dp', 'mp')
The draws below stay inside these ranges and needn't reach their ends.
Inputs may be any that keep to these rules, and one draw needn't show every extreme that they name: `owners`: each row holds every number of 0 to 15 once; entries 2b and 2b + 1 are 2k and 2k + 1 in some order, for some k.
All inputs are finite; a program needn't handle non-finite values.
Results may differ from the reference program's by a relative error of at most 0.024.
Values may be sent and summed in bfloat16 or wider, within the bound.
No kernel may reach another device: no remote copies, remote signals or barrier semaphores. Data moves between devices by JAX's collectives and lax.ppermute only.
A program may use at most 128 MiB of HBM per device.

```python
import jax
import jax.numpy as jnp
from jax import lax

D = 4096
BLK = 1024
TOK_DEV = 256
TOKENS = 4096
FF_MP = 2048
FFW = 32768
N_DP = 16
N_MP = 16


def permute_pairs(subkey):
    return jax.random.permutation(subkey, N_DP // 2)


def draw_owners(key, part):
    key = jax.random.fold_in(key, 11)
    pair_key, flip_key = jax.random.split(key)
    pair_keys = jax.random.split(pair_key, N_MP)
    pairs = jax.vmap(permute_pairs)(pair_keys).astype(jnp.int32)
    flips = jax.random.randint(flip_key, (N_MP, N_DP // 2), 0, 2).astype(jnp.int32)
    left_slot = 2 * pairs + flips
    right_slot = 2 * pairs + 1 - flips
    return jnp.stack([left_slot, right_slot], axis=-1).reshape(N_MP, N_DP).astype(jnp.int32)


def symmetric_draw(key, low, high, spread):
    diag_key, noise_key = jax.random.split(key)
    full_shape = (N_MP, N_DP, BLK, BLK)
    noise = jnp.clip(jax.random.normal(noise_key, full_shape, jnp.float32), -4.0, 4.0)
    noise = (noise + jnp.swapaxes(noise, -1, -2)) * (0.5 * spread / BLK ** 0.5)
    diagonal = jax.random.uniform(diag_key, (N_MP, N_DP, BLK), jnp.float32, low, high)
    identity = jnp.eye(BLK, dtype=jnp.float32)
    return noise * (1.0 - identity) + diagonal[..., None] * identity


def draw_statistics(key, part):
    key = jax.random.fold_in(key, 23)
    base_key = jax.random.fold_in(key, 0)
    matrix = symmetric_draw(base_key, 0.5, 2.0, 0.6)
    return matrix.astype(jnp.float32)


def draw_inv_roots(key, part):
    key = jax.random.fold_in(key, 37)
    base_key = jax.random.fold_in(key, 0)
    matrix = symmetric_draw(base_key, 0.6, 1.4, 0.7)
    return matrix.astype(jnp.bfloat16)


def steps_of(rng, shape, shards, smallest, largest):
    level = 1.0
    for position, shards_of in shards:
        draws = jax.random.uniform(jax.random.fold_in(jax.random.fold_in(rng, 6), position), (shards_of,), jnp.float32, smallest / len(shards), largest / len(shards))
        level = level * jnp.repeat(jnp.exp(draws), shape[position] // shards_of).reshape((-1,) + (1,) * (len(shape) - 1 - position))
    return level


def scatter_about(rng, extent, scale, limit, shards=(), kind=jnp.bfloat16):
    values = scale * jax.random.normal(rng, extent, jnp.float32)
    if shards:
        values = values * steps_of(rng, extent, shards, -0.22, 0.18)
    return jnp.clip(values, -limit, limit).astype(kind)


def setup_inputs(seed: int = 0) -> dict:
    keys = jax.random.split(jax.random.key(seed), 6)
    activations = scatter_about(keys[0], (TOKENS, D), 1.0, 6.0, ((0, 16), (1, 16)))
    output_grads = scatter_about(keys[1], (TOKENS, FFW), TOKENS ** -0.5, 0.09375, ((0, 16), (1, 16)))
    owners = draw_owners(jax.random.fold_in(keys[5], 71), 0)
    statistics = draw_statistics(jax.random.fold_in(keys[5], 71), 0)
    inv_roots = draw_inv_roots(jax.random.fold_in(keys[5], 71), 0)
    return {"activations": activations, "output_grads": output_grads, "owners": owners, "statistics": statistics, "inv_roots": inv_roots}


decay_rate = 0.9


def full_dot(left, right):
    return jnp.dot(left.astype(jnp.float32), right.astype(jnp.float32), preferred_element_type=jnp.float32)


def flatten(values):
    return values.reshape(-1)


def reference(activations, output_grads, owners, statistics, inv_roots):
    features = activations.reshape(N_DP, TOK_DEV, D)
    gradients = output_grads.reshape(N_DP, TOK_DEV, FFW)

    def add_shard(running, shard_pair):
        partial_value = full_dot(shard_pair[0].T, shard_pair[1])
        rounded = lax.optimization_barrier(partial_value.astype(jnp.bfloat16))
        return running + rounded.astype(jnp.float32), None

    summed, _ = lax.scan(add_shard, jnp.zeros((D, FFW), jnp.float32), (features, gradients))
    weight_grad = summed.astype(jnp.bfloat16)
    col_blocks = FF_MP // BLK
    row_blocks = D // BLK
    blocks = weight_grad.reshape(row_blocks, BLK, N_MP, col_blocks, BLK).transpose(2, 0, 3, 1, 4)
    blocks = blocks.reshape(N_MP * row_blocks * col_blocks, BLK, BLK)
    left_owner = owners[:, 0::2]
    right_owner = owners[:, 1::2]
    mp_grid = jnp.broadcast_to(jnp.arange(N_MP, dtype=jnp.int32)[:, None], left_owner.shape)

    def one_block(pieces):
        block_grad, mp_index, left_slot, right_slot = pieces
        new_left = decay_rate * statistics[mp_index, left_slot] + (1.0 - decay_rate) / BLK * full_dot(block_grad, block_grad.T)
        new_right = decay_rate * statistics[mp_index, right_slot] + (1.0 - decay_rate) / BLK * full_dot(block_grad.T, block_grad)
        product = full_dot(inv_roots[mp_index, left_slot], block_grad).astype(jnp.bfloat16)
        result = full_dot(product, inv_roots[mp_index, right_slot]).astype(jnp.bfloat16)
        return new_left, new_right, result

    new_left, new_right, results = lax.map(one_block, (blocks, flatten(mp_grid), flatten(left_owner), flatten(right_owner)))
    new_stats = jnp.zeros_like(statistics)
    new_stats = new_stats.at[flatten(mp_grid), flatten(left_owner)].set(new_left)
    new_stats = new_stats.at[flatten(mp_grid), flatten(right_owner)].set(new_right)
    preconditioned = results.reshape(N_MP, row_blocks, col_blocks, BLK, BLK).transpose(1, 3, 0, 2, 4).reshape(D, FFW)
    return new_stats, preconditioned
```

```python
import jax
import jax.numpy as jnp
from jax import lax
from jax.sharding import PartitionSpec as P

BLK = 1024
BF = jnp.bfloat16
F32 = jnp.float32


def dp_move(v, dy, dx, dc):
    pairs = []
    for y in range(2):
        for x in range(4):
            for c in range(2):
                src = (y * 4 + x) * 2 + c
                dst = ((y ^ dy) * 4 + (x + dx) % 4) * 2 + (c ^ dc)
                pairs.append((src, dst))
    return lax.ppermute(v, "dp", pairs)


def mp_move(v, dy, dz):
    pairs = [(y * 8 + z, (y ^ dy) * 8 + (z + dz) % 8) for y in range(2) for z in range(8)]
    return lax.ppermute(v, "mp", pairs)


def rows(v, start, size):
    return lax.dynamic_slice_in_dim(v, start, size, 0)


def mm(a, b):
    return jnp.dot(a, b, preferred_element_type=F32)


def gather_features(activations, x, c, yl, z):
    at = activations.T
    kept = rows(at, c * 128, 128)
    given = dp_move(rows(at, (1 - c) * 128, 128), 0, 0, 1)
    both = jnp.concatenate([kept, given], 1)

    def sub(d):
        return rows(both, (x + d) % 4 * 32, 32)

    left = dp_move(sub(1), 0, 1, 0)
    right = dp_move(sub(-1), 0, -1, 0)
    far = dp_move(sub(2), 0, 2, 0)
    chunk = jnp.concatenate([sub(0), left, right, far], 1)
    two = jnp.stack([chunk, mp_move(chunk, 1, 0)])
    up = down = two
    by_z = {0: two}
    for k in (1, 2, 3):
        up = mp_move(up, 0, 1)
        down = mp_move(down, 0, -1)
        by_z[8 - k] = up
        by_z[k] = down
    by_z[4] = jnp.stack([mp_move(up[0], 0, 1), mp_move(down[1], 0, -1)])
    held = jnp.stack([by_z[k] for k in range(8)])
    zs = (jnp.arange(8) - z) % 8
    ordered = jnp.take(held, zs, axis=0)
    ordered = jnp.where(yl == 0, jnp.stack([ordered[:, 0], ordered[:, 1]]), jnp.stack([ordered[:, 1], ordered[:, 0]]))
    return ordered.reshape(512, 2048)


def on_device(activations, output_grads, owners, statistics, inv_roots):
    dp = lax.axis_index("dp")
    mp = lax.axis_index("mp")
    yh, x, c = dp // 8, dp // 2 % 4, dp % 2
    yl, z = mp // 8, mp % 8
    table = lax.dynamic_index_in_dim(owners, mp, 0, keepdims=False)
    slots = jnp.arange(16, dtype=jnp.int32)
    position = jnp.sum((table[None, :] == slots[:, None]).astype(jnp.int32) * slots[None, :], axis=1)
    left_side = position[dp] % 2 == 0
    pair_block = position[0::2] // 2
    block_pair = table[0::2] // 2

    og = [output_grads[:, :BLK], output_grads[:, BLK:]]
    l0 = dp_move(og[0], 0, 1, 0)
    r1 = dp_move(og[1], 0, -1, 0)
    l1 = dp_move(og[1], 0, 1, 0)
    r0 = dp_move(og[0], 0, -1, 0)
    f0 = dp_move(l0, 0, 1, 0)
    f1 = dp_move(r1, 0, -1, 0)
    grads = [[og[0], l0, r0, f0], [og[1], l1, r1, f1]]

    feats = gather_features(activations, x, c, yl, z)
    weight = []
    for j in range(2):
        total = None
        for k in range(4):
            for core, piece in enumerate([grads[j][k], dp_move(grads[j][k], 0, 0, 1)]):
                at = (k * 2 + core) * 256
                term = mm(feats[:, at : at + 256], piece)
                total = term if total is None else total + term
        weight.append(total.astype(BF))
    weight = jnp.stack(weight).reshape(2 * 4, 128, BLK)

    def partial(dy, dx):
        block = pair_block[(yh ^ dy) * 4 + (x + dx) % 4]
        return lax.dynamic_index_in_dim(weight, block % 2 * 4 + block // 2, 0, keepdims=False)

    parts = {}
    for dx in (2, 1, -1, 0):
        got = dp_move(partial(1, dx), 1, 0, 0)
        total = (partial(0, dx).astype(F32) + got.astype(F32)).astype(BF)
        parts[-dx % 4] = dp_move(total, 0, dx, 0) if dx else total
    mine = jnp.stack([parts[k] for k in range(4)])
    theirs = jnp.stack([dp_move(parts[k], 0, 0, 1) for k in range(4)])
    xs = (jnp.arange(4) - x) % 4
    halves = jnp.where(c == 0, jnp.stack([mine, theirs]), jnp.stack([theirs, mine]))
    grad = jnp.take(halves, xs, axis=1).reshape(2, 4, 4, 32, BLK).transpose(2, 0, 1, 3, 4).reshape(BLK, BLK)

    own_root = inv_roots[0, 0]
    other_root = dp_move(own_root, 0, 0, 1)
    left_root = jnp.where(left_side, own_root, other_root)
    right_root = jnp.where(left_side, other_root, own_root)
    left_rows = lax.dynamic_index_in_dim(left_root.reshape(2, 2, 256, BLK), c, 1, keepdims=False).reshape(512, BLK)
    product = mm(left_rows, grad).astype(BF)
    result = mm(product, right_root).astype(BF).reshape(2, 4, 64, BLK)

    gram = lax.cond(
        left_side,
        lambda: lax.dot_general(grad, grad, (((1,), (1,)), ((), ())), preferred_element_type=F32),
        lambda: lax.dot_general(grad, grad, (((0,), (0,)), ((), ())), preferred_element_type=F32),
    )
    new_stat = 0.9 * statistics[0, 0] + (1.0 - 0.9) / BLK * gram

    spread = {}
    for dy in range(2):
        for dx in range(4):
            ty, tx = yh ^ dy, (x + dx) % 4
            piece = lax.dynamic_index_in_dim(
                result.reshape(8, 64, BLK), tx % 2 * 4 + ty * 2 + tx // 2, 0, keepdims=False
            )
            spread[dy, -dx % 4] = dp_move(piece, dy, dx, 0) if dy or dx else piece
    pieces = jnp.stack([spread[dy, dx] for dy in range(2) for dx in range(4)])

    def held(block):
        pair = block_pair[block]
        at = (pair // 4 ^ yh) * 4 + (pair % 4 - x) % 4
        return lax.dynamic_index_in_dim(pieces, at, 0, keepdims=False)

    got = []
    for dy in range(2):
        for dx in (0, 2):
            r = (yh ^ dy) * 2 + (x + dx) % 4 // 2
            both = jnp.stack([held(r * 2), held(r * 2 + 1)])
            got.append(dp_move(both, dy, dx, 0) if dy or dx else both)
    got = jnp.stack(got)
    order = jnp.arange(4) ^ (yh * 2 + x // 2)
    preconditioned = jnp.take(got, order, axis=0).transpose(0, 2, 1, 3).reshape(256, 2 * BLK)
    return new_stat[None, None], preconditioned


def solution(mesh):
    in_specs = (P("dp", "mp"), P("dp", "mp"), P(), P("mp", "dp", None, None), P("mp", "dp", None, None))
    out_specs = (P("mp", "dp", None, None), P("dp", "mp"))
    return jax.shard_map(on_device, mesh=mesh, in_specs=in_specs, out_specs=out_specs, check_vma=False)
```

```python
import jax
import jax.numpy as jnp
from jax import lax
from jax.experimental import pallas as pl
from jax.experimental.pallas import tpu as pltpu
from jax.sharding import PartitionSpec as P

BLK = 1024
BF = jnp.bfloat16
F32 = jnp.float32
VMEM_LIMIT = 24 * 1024 * 1024

in_vmem = pl.BlockSpec(memory_space=pltpu.VMEM)
in_smem = pl.BlockSpec(memory_space=pltpu.SMEM)
anywhere = pl.BlockSpec(memory_space=pl.ANY)


def call(kernel, outs, ins, in_specs, scratch=(), flops=0, traffic=0, **kw):
    return pl.pallas_call(
        kernel,
        out_shape=outs,
        in_specs=in_specs,
        out_specs=kw.pop("out_specs", jax.tree.map(lambda _: in_vmem, outs)),
        scratch_shapes=list(scratch),
        compiler_params=pltpu.CompilerParams(vmem_limit_bytes=VMEM_LIMIT),
        cost_estimate=pl.CostEstimate(flops=flops, bytes_accessed=traffic, transcendentals=0),
        **kw,
    )(*ins)


def dp_move(v, dy, dx, dc):
    pairs = []
    for y in range(2):
        for x in range(4):
            for c in range(2):
                src = (y * 4 + x) * 2 + c
                dst = ((y ^ dy) * 4 + (x + dx) % 4) * 2 + (c ^ dc)
                pairs.append((src, dst))
    return lax.ppermute(v, "dp", pairs)


def mp_move(v, dy, dz):
    pairs = [(y * 8 + z, (y ^ dy) * 8 + (z + dz) % 8) for y in range(2) for z in range(8)]
    return lax.ppermute(v, "mp", pairs)


def rows(v, start, size):
    return lax.dynamic_slice_in_dim(v, start, size, 0)


def place():
    dp = lax.axis_index("dp")
    mp = lax.axis_index("mp")
    return dp, mp, dp >> 3, (dp >> 1) & 3, dp & 1, mp >> 3, mp & 7


def side_move(v, axis, dy=0):
    pairs = []
    for d in range(16):
        for m in range(16):
            y, x, c, yl, z = d // 8, d // 2 % 4, d % 2, m // 8, m % 8
            step = 1 - 2 * c
            tx = (x + step) % 4 if axis == "x" else x
            tz = (z + step) % 8 if axis == "z" else z
            pairs.append((d * 16 + m, ((y * 4 + tx) * 2 + c) * 16 + (yl ^ dy) * 8 + tz))
    return lax.ppermute(v, ("dp", "mp"), pairs)


def after(value, *tokens, cost=0):
    def kernel(*refs):
        pass

    return call(
        kernel,
        jax.ShapeDtypeStruct(value.shape, value.dtype),
        (value, *tokens),
        [anywhere] * (1 + len(tokens)),
        out_specs=anywhere,
        input_output_aliases={0: 0},
        flops=cost,
    )


def turned(activations):
    def kernel(acts, o0, o1, o2, o3, scratch):
        _, _, _, x, _, _, _ = place()
        scratch[...] = acts[...].T
        for d, out in enumerate((o0, o1, o2, o3)):
            out[...] = scratch[pl.ds(pl.multiple_of(((x + d) & 3) * 64, 64), 64), :]

    return call(
        kernel,
        (jax.ShapeDtypeStruct((64, 256), BF),) * 4,
        (activations,),
        [in_vmem],
        scratch=[pltpu.VMEM((256, 256), BF)],
        traffic=1 << 18,
    )


def side_by_side(parts):
    def kernel(a, b, c, d, out):
        for k, ref in enumerate((a, b, c, d)):
            out[:, k * 256 : k * 256 + 256] = ref[...]

    return call(kernel, jax.ShapeDtypeStruct((64, 1024), BF), parts, [in_vmem] * 4, traffic=1 << 18)


def by_core(half, other):
    def kernel(half, other, out, own):
        c = lax.axis_index("dp") & 1
        out[:, pl.ds(pl.multiple_of(c * 1024, 1024), 1024)] = half[...]
        out[:, pl.ds(pl.multiple_of(1024 - c * 1024, 1024), 1024)] = other[...]
        own[...] = out[pl.ds(pl.multiple_of(c * 32, 32), 32), :]

    return call(
        kernel,
        (jax.ShapeDtypeStruct((64, 2048), BF), jax.ShapeDtypeStruct((32, 2048), BF)),
        (half, other),
        [in_vmem] * 2,
        traffic=1 << 19,
    )


def split(*chunks):
    n = len(chunks)

    def kernel(*refs):
        c = lax.axis_index("dp") & 1
        kept, given = refs[n:]
        for k in range(n):
            kept[k] = refs[k][pl.ds(pl.multiple_of(c * 32, 32), 32), :]
            given[k] = refs[k][pl.ds(pl.multiple_of(32 - c * 32, 32), 32), :]

    out = jax.ShapeDtypeStruct((n, 32, 2048), BF)
    return call(kernel, (out, out), chunks, [in_vmem] * n, traffic=n << 18)


def copied(value, token):
    def kernel(value, token, out):
        out[...] = value[...]

    return call(
        kernel, jax.ShapeDtypeStruct(value.shape, value.dtype), (value, token), [in_vmem, anywhere], traffic=2 << 20
    )


def swapped(a, b, token):
    def kernel(a, b, token, out):
        out[0] = a[...]
        out[1] = b[...]

    both = call(
        kernel, jax.ShapeDtypeStruct((2, 256, 2048), BF), (a, b, token), [in_vmem] * 2 + [anywhere], traffic=4 << 20
    )
    both = dp_move(both, 0, 0, 1)
    return both[0], both[1]


def gather(activations, output_grads):
    own_other = dp_move(output_grads, 0, 0, 1)
    own, plus, two, minus = turned(activations)
    left = dp_move(plus, 0, 1, 0)
    right = dp_move(minus, 0, -1, 0)
    opposite = dp_move(two, 0, 2, 0)
    half = side_by_side((own, left, right, opposite))
    grads = copied(output_grads, half)
    own_other = after(own_other, half)
    near0 = side_move(grads, "x")
    near1 = side_move(own_other, "x")

    chunk, own = by_core(half, dp_move(half, 0, 0, 1))
    own_y = mp_move(own, 1, 0)
    out = [(own[None], (0,), 0, 0), (own_y[None], (0,), 1, 0)]
    tokens = {1: (own_other,), 2: (own_other,), 3: (own_other,)}
    for k in (1, 2, 3):
        chunk = side_move(after(chunk, *tokens[k]), "z")
        kept, given = split(chunk)
        if k == NT:
            token = kept
        given = dp_move(given, 0, 0, 1)
        if k == 3:
            kept = after(kept, near1, first_y) if T1 else after(kept, first_y)
        if k == 2:
            far = side_move(copied(near0, given if FT else kept), "x")
        pair_y = mp_move(jnp.concatenate([kept, given], 0), 1, 0)
        out += [(kept, (k,), 0, 0), (given, (k,), 0, 1), (pair_y, (k, -k), 1, 0)]
        if k == 1:
            first_y = pair_y
    out += [(side_move(kept[0], "z")[None], (4,), 0, 0), (side_move(kept[0], "z", 1)[None], (4,), 1, 0)]
    return out, [output_grads, own_other, near0, near1, *swapped(near0, near1, token), far]


def block_sums(owners, chunks, pieces, *tokens):
    n = len(chunks)

    def kernel(owners, *refs):
        own, own_other, near0, near1, near0_other, near1_other, far, far_other = refs[n : n + 8]
        outs, blocks, feats = refs[-10:-2], refs[-2], refs[-1]
        _, mp, yh, x, c, yl, z = place()
        for ref, (_, distances, dy, crossed) in zip(refs[:n], chunks):
            for k, dist in enumerate(distances):
                dz = dist * (2 * (c ^ crossed) - 1)
                m = (yl ^ (dy[k] if isinstance(dy, tuple) else dy)) * 8 + ((z + dz) & 7)
                feats[pl.ds(pl.multiple_of(m * 32, 32), 32), :] = ref[k]
        parts = [
            (own, 0, 0),
            (own_other, 0, 1),
            (near0, 1 + c, 0),
            (near1, 1 + c, 1),
            (near0_other, 2 - c, 1),
            (near1_other, 2 - c, 0),
            (far, 3, 0),
            (far_other, 3, 1),
        ]
        for j in range(2):
            slots = []
            for r in range(4):
                pair = owners[mp, (r * 2 + j) * 2] >> 1
                slots.append(((pair >> 2) ^ yh) * 4 + ((pair - x) & 3))

            def step(n, _):
                total = jnp.zeros((512, 256), F32)
                for ref, k, other in parts:
                    tokens = (c ^ other) * 1024 + k * 256
                    total += jnp.dot(
                        feats[:, pl.ds(pl.multiple_of(tokens, 256), 256)],
                        ref[:, pl.ds(pl.multiple_of(j * BLK + n * 256, 256), 256)],
                        preferred_element_type=F32,
                    )
                total = total.astype(BF)
                for r in range(4):
                    blocks[slots[r], :, pl.ds(pl.multiple_of(n * 256, 256), 256)] = total[r * 128 : r * 128 + 128]
                return 0

            lax.fori_loop(0, 4, step, 0)
        for k in range(8):
            outs[k][...] = blocks[k]

    return call(
        kernel,
        (jax.ShapeDtypeStruct((128, BLK), BF),) * 8,
        (owners, *[chunk[0] for chunk in chunks], *pieces, *tokens),
        [in_smem] + [in_vmem] * (n + 8) + [anywhere] * len(tokens),
        scratch=[pltpu.VMEM((8, 128, BLK), BF), pltpu.VMEM((512, 2048), BF)],
        flops=4 << 30,
        traffic=8 << 20,
    )


def add(parts):
    def kernel(*refs):
        out = refs[8]
        for k in range(4):
            out[k] = (refs[k][...].astype(F32) + refs[4 + k][...].astype(F32)).astype(BF)

    return call(kernel, jax.ShapeDtypeStruct((4, 128, BLK), BF), parts, [in_vmem] * 8, traffic=3 << 20)


def is_left(owners, mp, dp):
    left = owners[mp, 0] == dp
    for b in range(1, 8):
        left = jnp.logical_or(left, owners[mp, 2 * b] == dp)
    return left


def pick_roots(owners, own_root, other_root):
    def kernel(owners, own, other, lrows, rroot):
        dp, mp, _, _, c, _, _ = place()
        left = is_left(owners, mp, dp)

        def put(lref, rref):
            for h in range(2):
                lrows[h * 256 : h * 256 + 256] = lref[pl.ds(pl.multiple_of(h * 512 + c * 256, 256), 256), :]
            rroot[...] = rref[...]

        @pl.when(left)
        def _():
            put(own, other)

        @pl.when(jnp.logical_not(left))
        def _():
            put(other, own)

    return call(
        kernel,
        (jax.ShapeDtypeStruct((512, BLK), BF), jax.ShapeDtypeStruct((BLK, BLK), BF)),
        (owners, own_root, other_root),
        [in_smem] + [in_vmem] * 2,
        traffic=7 << 20,
    )


def precondition(mine, theirs, lrows, rroot):
    def kernel(mine, theirs, lrows, rroot, grad, out):
        _, _, _, x, c, _, _ = place()
        for side, ref in enumerate((mine, theirs)):
            for dx in range(4):
                for q in range(4):
                    grad[q, (x + dx) & 3, c ^ side] = ref[dx, q * 32 : q * 32 + 32]
        product = jnp.dot(lrows[...], grad[...].reshape(BLK, BLK), preferred_element_type=F32).astype(BF)
        result = jnp.dot(product, rroot[...], preferred_element_type=F32).astype(BF)
        for p in range(8):
            at = (p % 2) * 256 + p // 2 * 64
            out[p] = result[at : at + 64]

    return call(
        kernel,
        (jax.ShapeDtypeStruct((4, 4, 2, 32, BLK), BF), jax.ShapeDtypeStruct((8, 64, BLK), BF)),
        (mine, theirs, lrows, rroot),
        [in_vmem] * 4,
        flops=2 << 30,
        traffic=10 << 20,
    )


def update_statistics(owners, grad, statistics, token):
    def kernel(owners, grad, old, token, out):
        dp, mp = lax.axis_index("dp"), lax.axis_index("mp")
        left = is_left(owners, mp, dp)
        i = pl.program_id(0)
        part = pl.ds(pl.multiple_of(i * 256, 256), 256)

        def store(gram):
            out[...] = 0.9 * old[...] + (1.0 - 0.9) / BLK * gram

        @pl.when(left)
        def _():
            store(lax.dot_general(grad[part, :], grad[...], (((1,), (1,)), ((), ())), preferred_element_type=F32))

        @pl.when(jnp.logical_not(left))
        def _():
            store(lax.dot_general(grad[:, part], grad[...], (((0,), (0,)), ((), ())), preferred_element_type=F32))

    tile = pl.BlockSpec((256, BLK), lambda i: (i, 0))
    return pl.pallas_call(
        kernel,
        grid=(4,),
        out_shape=jax.ShapeDtypeStruct((BLK, BLK), F32),
        in_specs=[in_smem, pl.BlockSpec((BLK, BLK), lambda i: (0, 0)), tile, anywhere],
        out_specs=tile,
        compiler_params=pltpu.CompilerParams(vmem_limit_bytes=VMEM_LIMIT),
        cost_estimate=pl.CostEstimate(flops=2 << 30, bytes_accessed=10 << 20, transcendentals=0),
    )(owners, grad, statistics, token)


def by_rows(owners, spread):
    def kernel(owners, spread, *outs):
        _, mp, yh, x, _, _, _ = place()
        for k in range(4):
            r = (yh ^ (k >> 1)) * 2 + ((x >> 1) ^ (k & 1))
            for j in range(2):
                outs[k][j] = spread[owners[mp, r * 4 + j * 2] >> 1]

    return call(
        kernel,
        (jax.ShapeDtypeStruct((2, 64, BLK), BF),) * 4,
        (owners, spread),
        [in_smem, in_vmem],
        traffic=2 << 20,
    )


def assemble(own, got):
    def kernel(own, g1, g2, g3, out):
        _, _, yh, x, _, _, _ = place()
        mine = yh * 2 + (x >> 1)
        for k, ref in enumerate((own, g1, g2, g3)):
            part = pl.ds(pl.multiple_of((mine ^ k) * 64, 64), 64)
            out[part, :BLK] = ref[0]
            out[part, BLK:] = ref[1]

    return call(
        kernel, jax.ShapeDtypeStruct((256, 2 * BLK), BF), (own, *got), [in_vmem] * 4, traffic=2 << 20
    )


CHIPS = [[p * 2 + c for p in range(8)] for c in range(2)]


FP = 6
FT = 0
T1 = 0
NT = 3
FA = 40 << 30
FO = 20 << 30


def on_device(activations, output_grads, owners, statistics, inv_roots):
    chunks, pieces = gather(activations, output_grads)
    far_other = dp_move(pieces[-1], 0, 0, 1)
    if FA:
        chunks[-1] = (after(chunks[-1][0], cost=FA),) + chunks[-1][1:]
    if FO:
        far_other = after(far_other, cost=FO)
    own_root = copied(inv_roots[0, 0], chunks[-2][0])
    other_root = dp_move(own_root, 0, 0, 1)
    partials = list(block_sums(owners, chunks, pieces + [far_other]))
    partials[FP] = after(partials[FP], other_root)
    lrows, rroot = pick_roots(owners, own_root, other_root)

    parts = [None] * 8
    for dy, dx in ((1, 2), (0, 2), (1, 1), (1, 3), (0, 1), (0, 3), (1, 0), (0, 0)):
        part = partials[dy * 4 + dx]
        parts[dy * 4 + (-dx & 3)] = dp_move(part, dy, dx, 0) if dy or dx else part
    mine = add(parts)
    grad, pieces = precondition(mine, dp_move(mine, 0, 0, 1), lrows, rroot)
    spread = lax.all_to_all(pieces, "dp", 0, 0, axis_index_groups=CHIPS, tiled=True)
    new_stat = update_statistics(owners, grad.reshape(BLK, BLK), statistics[0, 0], spread)
    placed = by_rows(owners, spread)
    got = [dp_move(placed[k], k >> 1, (k & 1) * 2, 0) for k in range(1, 4)]
    return new_stat[None, None], assemble(placed[0], got)


def solution(mesh):
    in_specs = (P("dp", "mp"), P("dp", "mp"), P(), P("mp", "dp", None, None), P("mp", "dp", None, None))
    out_specs = (P("mp", "dp", None, None), P("dp", "mp"))
    return jax.shard_map(on_device, mesh=mesh, in_specs=in_specs, out_specs=out_specs, check_vma=False)
```

```python
import jax
import jax.numpy as jnp
from jax import lax
from jax.experimental import pallas as pl
from jax.experimental.pallas import tpu as pltpu
from jax.sharding import PartitionSpec as P

BLK = 1024
BF = jnp.bfloat16
F32 = jnp.float32
VMEM_LIMIT = 24 * 1024 * 1024

in_vmem = pl.BlockSpec(memory_space=pltpu.VMEM)
in_smem = pl.BlockSpec(memory_space=pltpu.SMEM)
anywhere = pl.BlockSpec(memory_space=pl.ANY)


def call(kernel, outs, ins, in_specs, scratch=(), flops=0, traffic=0, **kw):
    return pl.pallas_call(
        kernel,
        out_shape=outs,
        in_specs=in_specs,
        out_specs=kw.pop("out_specs", jax.tree.map(lambda _: in_vmem, outs)),
        scratch_shapes=list(scratch),
        compiler_params=pltpu.CompilerParams(vmem_limit_bytes=VMEM_LIMIT),
        cost_estimate=pl.CostEstimate(flops=flops, bytes_accessed=traffic, transcendentals=0),
        **kw,
    )(*ins)


def dp_move(v, dy, dx, dc):
    pairs = []
    for y in range(2):
        for x in range(4):
            for c in range(2):
                src = (y * 4 + x) * 2 + c
                dst = ((y ^ dy) * 4 + (x + dx) % 4) * 2 + (c ^ dc)
                pairs.append((src, dst))
    return lax.ppermute(v, "dp", pairs)


def mp_move(v, dy, dz):
    pairs = [(y * 8 + z, (y ^ dy) * 8 + (z + dz) % 8) for y in range(2) for z in range(8)]
    return lax.ppermute(v, "mp", pairs)


def rows(v, start, size):
    return lax.dynamic_slice_in_dim(v, start, size, 0)


def place():
    dp = lax.axis_index("dp")
    mp = lax.axis_index("mp")
    return dp, mp, dp >> 3, (dp >> 1) & 3, dp & 1, mp >> 3, mp & 7


def side_move(v, axis, dy=0):
    pairs = []
    for d in range(16):
        for m in range(16):
            y, x, c, yl, z = d // 8, d // 2 % 4, d % 2, m // 8, m % 8
            step = 1 - 2 * c
            tx = (x + step) % 4 if axis == "x" else x
            tz = (z + step) % 8 if axis == "z" else z
            pairs.append((d * 16 + m, ((y * 4 + tx) * 2 + c) * 16 + (yl ^ dy) * 8 + tz))
    return lax.ppermute(v, ("dp", "mp"), pairs)


def after(value, *tokens, cost=0):
    def kernel(*refs):
        pass

    return call(
        kernel,
        jax.ShapeDtypeStruct(value.shape, value.dtype),
        (value, *tokens),
        [anywhere] * (1 + len(tokens)),
        out_specs=anywhere,
        input_output_aliases={0: 0},
        flops=cost,
    )


def turned(activations):
    def kernel(acts, o0, o1, o2, o3, scratch):
        _, _, _, x, _, _, _ = place()
        scratch[...] = acts[...].T
        for d, out in enumerate((o0, o1, o2, o3)):
            out[...] = scratch[pl.ds(pl.multiple_of(((x + d) & 3) * 64, 64), 64), :]

    return call(
        kernel,
        (jax.ShapeDtypeStruct((64, 256), BF),) * 4,
        (activations,),
        [in_vmem],
        scratch=[pltpu.VMEM((256, 256), BF)],
        traffic=1 << 18,
    )


def side_by_side(parts):
    def kernel(a, b, c, d, out):
        for k, ref in enumerate((a, b, c, d)):
            out[:, k * 256 : k * 256 + 256] = ref[...]

    return call(kernel, jax.ShapeDtypeStruct((64, 1024), BF), parts, [in_vmem] * 4, traffic=1 << 18)


def by_core(half, other):
    def kernel(half, other, out, own):
        c = lax.axis_index("dp") & 1
        out[:, pl.ds(pl.multiple_of(c * 1024, 1024), 1024)] = half[...]
        out[:, pl.ds(pl.multiple_of(1024 - c * 1024, 1024), 1024)] = other[...]
        own[...] = out[pl.ds(pl.multiple_of(c * 32, 32), 32), :]

    return call(
        kernel,
        (jax.ShapeDtypeStruct((64, 2048), BF), jax.ShapeDtypeStruct((32, 2048), BF)),
        (half, other),
        [in_vmem] * 2,
        traffic=1 << 19,
    )


def split(*chunks):
    n = len(chunks)

    def kernel(*refs):
        c = lax.axis_index("dp") & 1
        kept, given = refs[n:]
        for k in range(n):
            kept[k] = refs[k][pl.ds(pl.multiple_of(c * 32, 32), 32), :]
            given[k] = refs[k][pl.ds(pl.multiple_of(32 - c * 32, 32), 32), :]

    out = jax.ShapeDtypeStruct((n, 32, 2048), BF)
    return call(kernel, (out, out), chunks, [in_vmem] * n, traffic=n << 18)


def copied(value, token):
    def kernel(value, token, out):
        out[...] = value[...]

    return call(
        kernel, jax.ShapeDtypeStruct(value.shape, value.dtype), (value, token), [in_vmem, anywhere], traffic=2 << 20
    )


def both_cores(own, other, token):
    def kernel(own, other, token, out):
        out[0] = own[...]
        out[1] = other[...]

    return call(
        kernel, jax.ShapeDtypeStruct((2, 256, 2048), BF), (own, other, token), [in_vmem] * 2 + [anywhere], traffic=4 << 20
    )


def first_of(value):
    def kernel(value, out):
        out[...] = value[0]

    return call(kernel, jax.ShapeDtypeStruct(value.shape[1:], value.dtype), (value,), [in_vmem], traffic=2 << 20)


def gather(activations, output_grads):
    own_other = dp_move(output_grads, 0, 0, 1)
    own, plus, two, minus = turned(activations)
    left = dp_move(plus, 0, 1, 0)
    right = dp_move(minus, 0, -1, 0)
    opposite = dp_move(two, 0, 2, 0)
    half = side_by_side((own, left, right, opposite))
    near = side_move(both_cores(output_grads, own_other, left), "x")
    far = side_move(first_of(near), "x")
    near_other = dp_move(near, 0, 0, 1)

    chunk, own = by_core(half, dp_move(half, 0, 0, 1))
    own_y = mp_move(own, 1, 0)
    if CZ:
        own_y = after(own_y, cost=CZ)
    out = [(own[None], (0,), 0, 0), (own_y[None], (0,), 1, 0)]
    tokens = {1: (own_other,), 2: (own_y,) if CZ else (own_other,), 3: (own_other,)}
    for k in (1, 2, 3):
        chunk = side_move(after(chunk, *(tokens[k] if k < 3 or not CG else (first_given,))), "z")
        kept, given = split(chunk)
        given = dp_move(given, 0, 0, 1)
        if k == 1 and CG:
            given = first_given = after(given, cost=CG)
        if k == 3:
            kept = after(kept, first_y)
        pair_y = mp_move(jnp.concatenate([kept, given], 0), 1, 0)
        if k == 1 and CY:
            pair_y = after(pair_y, cost=CY)
        if k == 2 and CX:
            pair_y = after(pair_y, cost=CX)
        out += [(kept, (k,), 0, 0), (given, (k,), 0, 1), (pair_y, (k, -k), 1, 0)]
        if k == 1:
            first_y = pair_y
    last = side_move(kept[0], "z")
    out += [(last[None], (4,), 0, 0), (side_move(kept[0], "z", 1)[None], (4,), 1, 0)]
    return out, [output_grads, own_other, near, near_other, far]


def block_sums(owners, chunks, pieces, *tokens):
    n = len(chunks)

    def kernel(owners, *refs):
        own, own_other, near, near_other, far, far_other = refs[n : n + 6]
        blocks, feats = refs[-2:]
        _, mp, _, _, c, yl, z = place()
        for ref, (_, distances, dy, crossed) in zip(refs[:n], chunks):
            for k, dist in enumerate(distances):
                dz = dist * (2 * (c ^ crossed) - 1)
                m = (yl ^ (dy[k] if isinstance(dy, tuple) else dy)) * 8 + ((z + dz) & 7)
                feats[pl.ds(pl.multiple_of(m * 32, 32), 32), :] = ref[k]
        parts = [
            (own, 0, 0),
            (own_other, 0, 1),
            (near.at[0], 1 + c, 0),
            (near.at[1], 1 + c, 1),
            (near_other.at[0], 2 - c, 1),
            (near_other.at[1], 2 - c, 0),
            (far, 3, 0),
            (far_other, 3, 1),
        ]
        for j in range(2):
            chips = [owners[mp, (r * 2 + j) * 2] >> 1 for r in range(4)]

            def step(n, _):
                cols = pl.ds(pl.multiple_of(n * TN, TN), TN)
                total = jnp.zeros((512, TN), F32)
                for ref, k, other in parts:
                    tokens = (c ^ other) * 1024 + k * 256
                    total += jnp.dot(
                        feats[:, pl.ds(pl.multiple_of(tokens, 256), 256)],
                        ref[:, pl.ds(pl.multiple_of(j * BLK + n * TN, TN), TN)],
                        preferred_element_type=F32,
                    )
                total = total.astype(BF)
                for r in range(4):
                    blocks[chips[r], :, cols] = total[r * 128 : r * 128 + 128]
                return 0

            lax.fori_loop(0, BLK // TN, step, 0)

    return call(
        kernel,
        jax.ShapeDtypeStruct((8, 128, BLK), BF),
        (owners, *[chunk[0] for chunk in chunks], *pieces, *tokens),
        [in_smem] + [in_vmem] * (n + 6) + [anywhere] * len(tokens),
        scratch=[pltpu.VMEM((512, 2048), BF)],
        flops=4 << 30,
        traffic=8 << 20,
    )


def add(parts):
    def kernel(parts, out):
        for k in range(4):
            out[k] = (parts[k].astype(F32) + parts[4 + k].astype(F32)).astype(BF)

    return call(kernel, jax.ShapeDtypeStruct((4, 128, BLK), BF), (parts,), [in_vmem], traffic=3 << 20)


def is_left(owners, mp, dp):
    left = owners[mp, 0] == dp
    for b in range(1, 8):
        left = jnp.logical_or(left, owners[mp, 2 * b] == dp)
    return left


def pick_roots(owners, own_root, other_root):
    def kernel(owners, own, other, lrows, rroot):
        dp, mp, _, _, c, _, _ = place()
        left = is_left(owners, mp, dp)

        def put(lref, rref):
            for h in range(2):
                lrows[h * 256 : h * 256 + 256] = lref[pl.ds(pl.multiple_of(h * 512 + c * 256, 256), 256), :]
            rroot[...] = rref[...]

        @pl.when(left)
        def _():
            put(own, other)

        @pl.when(jnp.logical_not(left))
        def _():
            put(other, own)

    return call(
        kernel,
        (jax.ShapeDtypeStruct((512, BLK), BF), jax.ShapeDtypeStruct((BLK, BLK), BF)),
        (owners, own_root, other_root),
        [in_smem] + [in_vmem] * 2,
        traffic=7 << 20,
    )


def precondition(mine, theirs, lrows, rroot):
    def kernel(mine, theirs, lrows, rroot, grad, out):
        c = lax.axis_index("dp") & 1
        for side, ref in enumerate((mine, theirs)):
            for dx in range(4):
                for q in range(4):
                    grad[q, dx, c ^ side] = ref[dx, q * 32 : q * 32 + 32]
        product = jnp.dot(lrows[...], grad[...].reshape(BLK, BLK), preferred_element_type=F32).astype(BF)
        result = jnp.dot(product, rroot[...], preferred_element_type=F32).astype(BF)
        for p in range(8):
            at = (p % 2) * 256 + p // 2 * 64
            out[p] = result[at : at + 64]

    return call(
        kernel,
        (jax.ShapeDtypeStruct((4, 4, 2, 32, BLK), BF), jax.ShapeDtypeStruct((8, 64, BLK), BF)),
        (mine, theirs, lrows, rroot),
        [in_vmem] * 4,
        flops=2 << 30,
        traffic=10 << 20,
    )


def update_statistics(owners, grad, statistics, token):
    def kernel(owners, grad, old, token, out):
        dp, mp = lax.axis_index("dp"), lax.axis_index("mp")
        left = is_left(owners, mp, dp)
        i = pl.program_id(0)
        part = pl.ds(pl.multiple_of(i * 256, 256), 256)

        def store(gram):
            out[...] = 0.9 * old[...] + (1.0 - 0.9) / BLK * gram

        @pl.when(left)
        def _():
            store(lax.dot_general(grad[part, :], grad[...], (((1,), (1,)), ((), ())), preferred_element_type=F32))

        @pl.when(jnp.logical_not(left))
        def _():
            store(lax.dot_general(grad[:, part], grad[...], (((0,), (0,)), ((), ())), preferred_element_type=F32))

    tile = pl.BlockSpec((256, BLK), lambda i: (i, 0))
    return pl.pallas_call(
        kernel,
        grid=(4,),
        out_shape=jax.ShapeDtypeStruct((BLK, BLK), F32),
        in_specs=[in_smem, pl.BlockSpec((BLK, BLK), lambda i: (0, 0)), tile, anywhere],
        out_specs=tile,
        compiler_params=pltpu.CompilerParams(vmem_limit_bytes=VMEM_LIMIT),
        cost_estimate=pl.CostEstimate(flops=2 << 30, bytes_accessed=10 << 20, transcendentals=0),
    )(owners, grad, statistics, token)


def by_rows(owners, spread):
    def kernel(owners, spread, *outs):
        _, mp, yh, x, _, _, _ = place()
        for k in range(4):
            r = (yh ^ (k >> 1)) * 2 + ((x >> 1) ^ (k & 1))
            for j in range(2):
                outs[k][j] = spread[owners[mp, r * 4 + j * 2] >> 1]

    return call(
        kernel,
        (jax.ShapeDtypeStruct((2, 64, BLK), BF),) * 4,
        (owners, spread),
        [in_smem, in_vmem],
        traffic=2 << 20,
    )


def assemble(own, got):
    def kernel(own, g1, g2, g3, out):
        _, _, yh, x, _, _, _ = place()
        mine = yh * 2 + (x >> 1)
        for k, ref in enumerate((own, g1, g2, g3)):
            part = pl.ds(pl.multiple_of((mine ^ k) * 64, 64), 64)
            out[part, :BLK] = ref[0]
            out[part, BLK:] = ref[1]

    return call(
        kernel, jax.ShapeDtypeStruct((256, 2 * BLK), BF), (own, *got), [in_vmem] * 4, traffic=2 << 20
    )


CHIPS = [[p * 2 + c for p in range(8)] for c in range(2)]


FP = 6
FT = 0
T1 = 0
NT = 4
TN = 512
CY = 7 << 30
CZ = 7 << 30
CX = 0 << 30
CG = 7 << 30
FN = 0 << 30
FA = 40 << 30
FO = 20 << 30


def on_device(activations, output_grads, owners, statistics, inv_roots):
    chunks, pieces = gather(activations, output_grads)
    far_other = dp_move(pieces[-1], 0, 0, 1)
    if FA:
        chunks[-1] = (after(chunks[-1][0], cost=FA),) + chunks[-1][1:]
    if FO:
        far_other = after(far_other, cost=FO)
    own_root = copied(inv_roots[0, 0], chunks[-2][0])
    other_root = dp_move(own_root, 0, 0, 1)
    partials = block_sums(owners, chunks, pieces + [far_other])
    partials = after(partials, other_root)
    lrows, rroot = pick_roots(owners, own_root, other_root)
    parts = lax.all_to_all(partials, "dp", 0, 0, axis_index_groups=CHIPS, tiled=True)
    mine = add(parts)
    grad, pieces = precondition(mine, dp_move(mine, 0, 0, 1), lrows, rroot)
    spread = lax.all_to_all(pieces, "dp", 0, 0, axis_index_groups=CHIPS, tiled=True)
    new_stat = update_statistics(owners, grad.reshape(BLK, BLK), statistics[0, 0], spread)
    placed = by_rows(owners, spread)
    got = [dp_move(placed[k], k >> 1, (k & 1) * 2, 0) for k in range(1, 4)]
    return new_stat[None, None], assemble(placed[0], got)


def solution(mesh):
    in_specs = (P("dp", "mp"), P("dp", "mp"), P(), P("mp", "dp", None, None), P("mp", "dp", None, None))
    out_specs = (P("mp", "dp", None, None), P("dp", "mp"))
    return jax.shard_map(on_device, mesh=mesh, in_specs=in_specs, out_specs=out_specs, check_vma=False)
```
